32 devices in a mesh: row: 4 (over x, core), col: 8 (over z, y).
Axes of the slice: x: 2, y: 2, z: 4, core: 2. Of those that a mesh axis runs over, the one named last changes fastest.
Arguments:
- row_factors: float32 [8, 512, 256], P('col', 'row'), may hold values from -1.5 to 1.5
- row_accum: float32 [8, 512, 256], P('col', 'row'), may hold values from 0.01 to 0.1
- row_marginals: int32 [8, 512], P('col'), may hold values from 256 to 4095
- col_factors: float32 [4, 8, 512, 256], P('row', 'col'), may hold values from -1.5 to 1.5
- col_accum: float32 [4, 8, 512, 256], P('row', 'col'), may hold values from 0.01 to 0.1
- col_marginals: int32 [4, 8, 512], P('row', 'col'), may hold values from 256 to 4095
- counts: int32 [2, 8, 512, 4, 512], P(None, 'col', None, 'row'), may hold values from 0 to 63, as said below
- plan: int32 [2], replicated, may hold values from 1 to 7, as said below
Outputs:
- new_rows: float32 [8, 512, 256], P('col', 'row')
- new_row_accum: float32 [8, 512, 256], P('col', 'row')
- new_columns: float32 [4, 8, 512, 256], P('row', 'col')
- new_column_accum: float32 [4, 8, 512, 256], P('row', 'col')
The draws below stay inside these ranges and needn't reach their ends.
Inputs may be any that keep to these rules, and one draw needn't show every extreme that they name: `counts`: zero means an unobserved pair. `plan`: equal on all devices; the masks of the rounds are distinct, and one round's mask is 7.
All inputs are finite; a program needn't handle non-finite values.
Results may differ from the reference program's by a relative error of at most 0.0003.
Values sent between devices are 32-bit elements; how exact they have to be, the bound alone decides.
No kernel may reach another device: no remote copies, remote signals or barrier semaphores. Data moves between devices by JAX's collectives and lax.ppermute only.
A program may use at most 64 MiB of HBM per device.

```python
import math
import jax
import jax.numpy as jnp
from jax import lax

D = 256
CB = 512
RB = 512
ROUNDS = 2
N_ROW = 4
N_COL = 8


def draw_counts(key, part):
    shape = (ROUNDS, N_COL, RB, N_ROW, CB)
    values = jax.random.randint(jax.random.fold_in(key, 11), shape, 1, 64)
    keep = jax.random.randint(jax.random.fold_in(key, 12), shape, 0, 5)
    return jnp.where(keep >= 2, values, 0).astype(jnp.int32)


def draw_plan(key, part):
    order = (jax.random.permutation(jax.random.fold_in(key, 21), N_COL - 1) + 1).astype(jnp.int32)
    places = jnp.arange(N_COL - 1, dtype=jnp.int32)
    where_top = jnp.sum(jnp.where(order == N_COL - 1, places, 0)).astype(jnp.int32)
    target = jax.random.randint(jax.random.fold_in(key, 22), (), 0, ROUNDS).astype(jnp.int32)
    moved = order[target]
    order = jnp.where(places == target, N_COL - 1, jnp.where(places == where_top, moved, order))
    return order[:ROUNDS].astype(jnp.int32)


def plant(entries, own_key, smallest, largest):
    index_at = [jax.random.randint(jax.random.fold_in(own_key, axis), (), 0, length) for axis, length in enumerate(entries.shape)]
    longest = entries.shape.index(max(entries.shape))
    neighbour = index_at[:longest] + [(index_at[longest] + 1) % entries.shape[longest]] + index_at[longest + 1:]
    return entries.at[tuple(index_at)].set(smallest).at[tuple(neighbour)].set(largest)


def block_scale(stream_key, extent, cuts, smallest, top_value):
    def one(position, shards_of):
        steps = jax.random.uniform(jax.random.fold_in(jax.random.fold_in(stream_key, 6), position), (shards_of,), jnp.float32, smallest / len(cuts), top_value / len(cuts))
        return jnp.repeat(jnp.exp(steps), extent[position] // shards_of).reshape((-1,) + (1,) * (len(extent) - position - 1))

    factor_of = one(*cuts[0])
    for cut in cuts[1:]:
        factor_of = factor_of * one(*cut)
    return factor_of


def bell_draw(rng, extent, width, reach, shards=(), kind=jnp.bfloat16):
    result = jax.random.normal(rng, extent, jnp.float32) * width
    if len(shards) > 0:
        result = block_scale(rng, extent, shards, -0.22, 0.18) * result
    return jnp.clip(result, min=-reach, max=reach).astype(kind)


def setup_inputs(seed: int = 0) -> dict:
    key_of = jax.random.split(jax.random.key(seed), 9)
    return {
        "row_factors": bell_draw(key_of[0], (N_COL, RB, D), 0.25, 1.5, ((0, 8), (1, 4)), jnp.float32),
        "row_accum": jnp.clip(jnp.exp(math.log(0.1) - 2.3025851 * jax.random.uniform(key_of[1], (N_COL, RB, D), jnp.float32) ** block_scale(key_of[1], (N_COL, RB, D), ((0, 8), (1, 4)), -0.2, 0.2)), 0.01, 0.1),
        "row_marginals": plant(jax.random.randint(key_of[2], (N_COL, RB), 256, 4096), jax.random.fold_in(key_of[2], 1), 256, 4095).astype(jnp.int32),
        "col_factors": bell_draw(key_of[3], (N_ROW, N_COL, CB, D), 0.25, 1.5, ((0, 4), (1, 8)), jnp.float32),
        "col_accum": jnp.clip(jnp.exp(math.log(0.1) - 2.3025851 * jax.random.uniform(key_of[4], (N_ROW, N_COL, CB, D), jnp.float32) ** block_scale(key_of[4], (N_ROW, N_COL, CB, D), ((0, 4), (1, 8)), -0.2, 0.2)), 0.01, 0.1),
        "col_marginals": plant(jax.random.randint(key_of[5], (N_ROW, N_COL, CB), 256, 4096), jax.random.fold_in(key_of[5], 1), 256, 4095).astype(jnp.int32),
        "counts": draw_counts(jax.random.fold_in(key_of[8], 71), 0),
        "plan": draw_plan(jax.random.fold_in(key_of[8], 71), 0),
    }


log_total = 11.5
learn_rate = 0.05

def tile_grad(counts_tile, pred, log_r, log_c, columns):
    target = jnp.log(jnp.maximum(counts_tile, 1).astype(jnp.float32)) + log_total - log_r - log_c
    confidence = 0.1 + 0.25 * jnp.sqrt(counts_tile.astype(jnp.float32))
    error = jnp.where(counts_tile > 0, confidence * (pred - target), jax.nn.sigmoid(pred - target))
    return error / columns

def reference(row_factors, row_accum, row_marginals, col_factors, col_accum, col_marginals, counts, plan):
    log_rows = jnp.log(row_marginals.astype(jnp.float32))
    held = jnp.swapaxes(col_factors, 0, 1)
    held_acc = jnp.swapaxes(col_accum, 0, 1)
    held_log = jnp.swapaxes(jnp.log(col_marginals.astype(jnp.float32)), 0, 1)
    highest = lax.Precision.HIGHEST
    for step in range(ROUNDS):
        source = jnp.bitwise_xor(jnp.arange(N_COL, dtype=jnp.int32), plan[step].astype(jnp.int32))
        held = held[source]
        held_acc = held_acc[source]
        held_log = held_log[source]
        tiles = counts[step]

        def one_block(items):
            w_rows, w_acc, l_rows, h_cols, h_acc, l_cols, tile = items
            pred = jnp.einsum('id,rkd->irk', w_rows, h_cols, precision=highest)
            error = tile_grad(tile, pred, l_rows[:, None, None], l_cols[None], CB)
            grad_w = jnp.einsum('irk,rkd->id', error, h_cols, precision=highest)
            grad_h = jnp.einsum('irk,id->rkd', error, w_rows, precision=highest)
            w_acc = w_acc + grad_w * grad_w
            w_rows = w_rows - learn_rate * grad_w / jnp.sqrt(w_acc)
            h_acc = h_acc + grad_h * grad_h
            h_cols = h_cols - learn_rate * grad_h / jnp.sqrt(h_acc)
            return (w_rows, w_acc, h_cols, h_acc)
        row_factors, row_accum, held, held_acc = lax.map(one_block, (row_factors, row_accum, log_rows, held, held_acc, held_log, tiles))
    return (row_factors, row_accum, jnp.swapaxes(held, 0, 1), jnp.swapaxes(held_acc, 0, 1))
```

```python
import jax
import jax.numpy as jnp
from jax import lax
from jax.sharding import PartitionSpec as P

log_total = 11.5
learn_rate = 0.05
highest = lax.Precision.HIGHEST
CHUNKS = 2


def move(value, axis, mask):
    pairs = [(source, source ^ mask) for source in range(lax.axis_size(axis))]
    return lax.ppermute(value, axis, pairs)


def dot(a, b, dims):
    return lax.dot_general(
        a, b, (dims, ((), ())), precision=highest, preferred_element_type=jnp.float32
    )


def tile_grad(counts_tile, pred, log_r, log_c, columns):
    target = jnp.log(jnp.maximum(counts_tile, 1).astype(jnp.float32)) + log_total - log_r - log_c
    confidence = 0.1 + 0.25 * jnp.sqrt(counts_tile.astype(jnp.float32))
    error = jnp.where(counts_tile > 0, confidence * (pred - target), jax.nn.sigmoid(pred - target))
    return error / columns


def adagrad(param, accum, grad):
    accum = accum + grad * grad
    return (param - learn_rate * grad / jnp.sqrt(accum), accum)


def row_sum_scatter(value):
    size = lax.axis_size("row")
    if size & (size - 1):
        return lax.psum_scatter(value, "row", scatter_dimension=0, tiled=True)
    me = lax.axis_index("row")
    blocks = value.reshape(size, value.shape[0] // size, value.shape[1])
    bits = size.bit_length() - 1
    for bit in range(bits):
        pairs = blocks.reshape(blocks.shape[0] // 2, 2, *blocks.shape[1:])
        mine = (me >> bit) & 1
        keep = lax.dynamic_index_in_dim(pairs, mine, 1, keepdims=False)
        send = lax.dynamic_index_in_dim(pairs, 1 - mine, 1, keepdims=False)
        blocks = keep + move(send, "row", 1 << bit)
    return blocks[0]


def row_gather(value):
    return lax.all_gather(value, "row", axis=0, tiled=True)


def fit(tile, whole, held, log_rows, held_log, columns):
    pred = dot(whole, held, ((1,), (1,)))
    error = tile_grad(tile, pred, log_rows[:, None], held_log[None, :], columns)
    return dot(error, whole, ((0,), (0,))), dot(error, held, ((1,), (0,)))


def split(value, axis=0):
    return jnp.split(value, CHUNKS, axis=axis)


def two_rounds(first, second, state):
    shard, shard_acc, log_rows, cols, col_acc, col_log, tiles = state
    top = lax.axis_size("col") // 2
    both = first ^ second
    tile_cols = cols.shape[0]
    cols, col_acc = split(cols), split(col_acc)

    held = [move(h, "col", first) for h in cols]
    held_log = split(move(col_log, "col", first))
    whole = row_gather(shard)
    tile = split(tiles[0], 1)
    grads, parts = zip(
        *[
            fit(tile[k], whole, held[k], log_rows, held_log[k], tile_cols)
            for k in range(CHUNKS)
        ]
    )
    if first & top:
        last_acc = [move(a, "col", both) for a in col_acc]
        if second & top:
            last = [move(h, "col", both) for h in cols]
        else:
            last = [move(h, "col", second) for h in held]
        last_grads = [move(g, "col", second) for g in grads]
        held, held_acc = zip(
            *[adagrad(last[k], last_acc[k], last_grads[k]) for k in range(CHUNKS)]
        )
    else:
        held_acc = [move(a, "col", first) for a in col_acc]
        held, held_acc = zip(*[adagrad(held[k], held_acc[k], grads[k]) for k in range(CHUNKS)])
        held = [move(h, "col", second) for h in held]
        held_acc = [move(a, "col", second) for a in held_acc]
    held_log = split(move(col_log, "col", both))
    shard, shard_acc = adagrad(shard, shard_acc, row_sum_scatter(sum(parts)))

    whole = row_gather(shard)
    tile = split(tiles[1], 1)
    grads, parts = zip(
        *[
            fit(tile[k], whole, held[k], log_rows, held_log[k], tile_cols)
            for k in range(CHUNKS)
        ]
    )
    held, held_acc = zip(*[adagrad(held[k], held_acc[k], grads[k]) for k in range(CHUNKS)])
    shard, shard_acc = adagrad(shard, shard_acc, row_sum_scatter(sum(parts)))
    return shard, shard_acc, jnp.concatenate(held), jnp.concatenate(held_acc)


def any_rounds(plan, state):
    shard, shard_acc, log_rows, held, held_acc, held_log, tiles = state
    masks = range(1, lax.axis_size("col"))
    for step in range(tiles.shape[0]):
        held, held_acc, held_log = lax.switch(
            plan[step] - 1,
            [lambda s, m=m: tuple(move(v, "col", m) for v in s) for m in masks],
            (held, held_acc, held_log),
        )
        whole = row_gather(shard)
        grad_cols, grad_rows = fit(tiles[step], whole, held, log_rows, held_log, held.shape[0])
        shard, shard_acc = adagrad(shard, shard_acc, row_sum_scatter(grad_rows))
        held, held_acc = adagrad(held, held_acc, grad_cols)
    return shard, shard_acc, held, held_acc


def per_device(
    row_factors, row_accum, row_marginals, col_factors, col_accum, col_marginals, counts, plan
):
    rounds, _, rows_block, _, tile_cols = counts.shape
    width = row_factors.shape[2]
    size = lax.axis_size("col")
    state = (
        row_factors[0],
        row_accum[0],
        jnp.log(row_marginals[0].astype(jnp.float32)),
        col_factors[0, 0],
        col_accum[0, 0],
        jnp.log(col_marginals[0, 0].astype(jnp.float32)),
        counts.reshape(rounds, rows_block, tile_cols),
    )
    if rounds == 2 and 4 <= size <= 8:
        full = size - 1
        pairs = [(full, m) for m in range(1, full)] + [(m, full) for m in range(1, full)]
        which = jnp.where(plan[0] == full, plan[1] - 1, plan[0] - 1 + full - 1)
        out = lax.switch(
            which,
            [lambda s, a=a, b=b: two_rounds(a, b, s) for a, b in pairs],
            state,
        )
    else:
        out = any_rounds(plan, state)
    shard, shard_acc, held, held_acc = out
    return (
        shard.reshape(1, -1, width),
        shard_acc.reshape(1, -1, width),
        held.reshape(1, 1, tile_cols, width),
        held_acc.reshape(1, 1, tile_cols, width),
    )


def solution(mesh):
    in_specs = (
        P("col", "row", None),
        P("col", "row", None),
        P("col", None),
        P("row", "col", None, None),
        P("row", "col", None, None),
        P("row", "col", None),
        P(None, "col", None, "row", None),
        P(),
    )
    out_specs = (
        P("col", "row", None),
        P("col", "row", None),
        P("row", "col", None, None),
        P("row", "col", None, None),
    )
    return jax.shard_map(
        per_device, mesh=mesh, in_specs=in_specs, out_specs=out_specs, check_vma=False
    )
```

```python
import jax
import jax.numpy as jnp
from jax import lax
from jax.sharding import PartitionSpec as P

log_total = 11.5
learn_rate = 0.05
highest = lax.Precision.HIGHEST


def move(value, axis, mask):
    pairs = [(source, source ^ mask) for source in range(lax.axis_size(axis))]
    return lax.ppermute(value, axis, pairs)


def dot(a, b, dims):
    return lax.dot_general(
        a, b, (dims, ((), ())), precision=highest, preferred_element_type=jnp.float32
    )


def tile_grad(counts_tile, pred, log_r, log_c, columns):
    target = jnp.log(jnp.maximum(counts_tile, 1).astype(jnp.float32)) + log_total - log_r - log_c
    confidence = 0.1 + 0.25 * jnp.sqrt(counts_tile.astype(jnp.float32))
    error = jnp.where(counts_tile > 0, confidence * (pred - target), jax.nn.sigmoid(pred - target))
    return error / columns


def adagrad(param, accum, grad):
    accum = accum + grad * grad
    return (param - learn_rate * grad / jnp.sqrt(accum), accum)


def row_sum_scatter(value):
    size = lax.axis_size("row")
    if size & (size - 1):
        return lax.psum_scatter(value, "row", scatter_dimension=0, tiled=True)
    me = lax.axis_index("row")
    blocks = value.reshape(size, value.shape[0] // size, value.shape[1])
    bits = size.bit_length() - 1
    for bit in range(bits):
        pairs = blocks.reshape(blocks.shape[0] // 2, 2, *blocks.shape[1:])
        mine = (me >> bit) & 1
        keep = lax.dynamic_index_in_dim(pairs, mine, 1, keepdims=False)
        send = lax.dynamic_index_in_dim(pairs, 1 - mine, 1, keepdims=False)
        blocks = keep + move(send, "row", 1 << bit)
    return blocks[0]


def row_gather(value):
    size = lax.axis_size("row")
    if size & (size - 1):
        return lax.all_gather(value, "row", axis=0, tiled=True)
    me = lax.axis_index("row")
    blocks = value[None]
    for bit in reversed(range(size.bit_length() - 1)):
        other = move(blocks, "row", 1 << bit)
        low = (me >> bit) & 1 == 0
        pairs = [jnp.where(low, blocks, other), jnp.where(low, other, blocks)]
        blocks = jnp.stack(pairs, axis=1).reshape(-1, *value.shape)
    return blocks.reshape(-1, value.shape[1])


def tile_error(tile, whole, held, log_rows, held_log):
    pred = dot(whole, held, ((1,), (1,)))
    return tile_grad(tile, pred, log_rows[:, None], held_log[None, :], held.shape[0])


def crosses(mask):
    return mask & (lax.axis_size("col") // 2) != 0


def before(first, second, state):
    shard, cols, acc, log_cols, counts = state
    rounds, _, rows_block, _, tile_cols = counts.shape
    both = first ^ second
    half = tile_cols // 2
    held = move(cols, "col", first)
    early, waiting = jnp.zeros_like(cols), jnp.zeros_like(acc[half:])
    if crosses(first):
        if crosses(second):
            early = move(acc, "col", both)
    else:
        early = move(jnp.concatenate([cols[:half], acc[:half]]), "col", both)
        waiting = move(acc[half:], "col", first)
    log_now = move(log_cols, "col", first)
    log_next = move(log_cols, "col", both)
    whole = row_gather(shard)
    return held, early, waiting, log_now, log_next, whole, counts.reshape(rounds, rows_block, tile_cols)


def between(first, second, state):
    shard, shard_acc, cols, acc, held, early, waiting, grad, grad_rows = state
    both = first ^ second
    half = cols.shape[0] // 2
    if crosses(first):
        grad = move(grad, "col", second)
        if crosses(second):
            last = move(cols, "col", both)
        else:
            last = move(held, "col", second)
            early = move(acc, "col", both)
        last, last_acc = adagrad(last, early, grad)
    else:
        later, waiting = adagrad(held[half:], waiting, grad[half:])
        sent = move(jnp.concatenate([grad[:half], later]), "col", second)
        front, front_acc = adagrad(early[:half], early[half:], sent[:half])
        last = jnp.concatenate([front, sent[half:]])
        last_acc = jnp.concatenate([front_acc, jnp.zeros_like(front_acc)])
    shard, shard_acc = adagrad(shard, shard_acc, row_sum_scatter(grad_rows))
    return shard, shard_acc, row_gather(shard), last, last_acc, waiting


def after(split, state):
    shard, shard_acc, whole, held, held_acc, waiting, error, grad_rows = state
    if split:
        half = waiting.shape[0]
        full = lax.axis_size("col") - 1
        held_acc = jnp.concatenate([held_acc[:half], move(waiting, "col", full)])
    held, held_acc = adagrad(held, held_acc, dot(error, whole, ((0,), (0,))))
    shard, shard_acc = adagrad(shard, shard_acc, row_sum_scatter(grad_rows))
    return shard, shard_acc, held, held_acc


def two_rounds(plan, shard, shard_acc, log_rows, cols, acc, log_cols, counts):
    full = lax.axis_size("col") - 1
    pairs = [(full, m) for m in range(1, full)] + [(m, full) for m in range(1, full)]
    which = jnp.where(plan[0] == full, plan[1] - 1, plan[0] - 1 + full - 1)

    def by_plan(step, state):
        return lax.switch(which, [lambda s, a=a, b=b: step(a, b, s) for a, b in pairs], state)

    held, early, waiting, log_now, log_next, whole, tiles = by_plan(
        before, (shard, cols, acc, log_cols, counts)
    )
    error = tile_error(tiles[0], whole, held, log_rows, log_now)
    grad = dot(error, whole, ((0,), (0,)))
    grad_rows = dot(error, held, ((1,), (0,)))
    shard, shard_acc, whole, held, held_acc, waiting = by_plan(
        between, (shard, shard_acc, cols, acc, held, early, waiting, grad, grad_rows)
    )
    error = tile_error(tiles[1], whole, held, log_rows, log_next)
    grad_rows = dot(error, held, ((1,), (0,)))
    crossing = plan[0] >= lax.axis_size("col") // 2
    return lax.cond(
        crossing,
        lambda s: after(False, s),
        lambda s: after(True, s),
        (shard, shard_acc, whole, held, held_acc, waiting, error, grad_rows),
    )


def any_rounds(plan, shard, shard_acc, log_rows, held, held_acc, held_log, counts):
    rounds, _, rows_block, _, tile_cols = counts.shape
    tiles = counts.reshape(rounds, rows_block, tile_cols)
    masks = range(1, lax.axis_size("col"))
    for step in range(rounds):
        held, held_acc, held_log = lax.switch(
            plan[step] - 1,
            [lambda s, m=m: tuple(move(v, "col", m) for v in s) for m in masks],
            (held, held_acc, held_log),
        )
        whole = row_gather(shard)
        error = tile_error(tiles[step], whole, held, log_rows, held_log)
        grad_rows = dot(error, held, ((1,), (0,)))
        grad_cols = dot(error, whole, ((0,), (0,)))
        shard, shard_acc = adagrad(shard, shard_acc, row_sum_scatter(grad_rows))
        held, held_acc = adagrad(held, held_acc, grad_cols)
    return shard, shard_acc, held, held_acc


def per_device(
    row_factors, row_accum, row_marginals, col_factors, col_accum, col_marginals, counts, plan
):
    width = row_factors.shape[2]
    tile_cols = col_factors.shape[2]
    few = counts.shape[0] == 2 and 4 <= lax.axis_size("col") <= 8
    shard, shard_acc, held, held_acc = (two_rounds if few else any_rounds)(
        plan,
        row_factors[0],
        row_accum[0],
        jnp.log(row_marginals[0].astype(jnp.float32)),
        col_factors[0, 0],
        col_accum[0, 0],
        jnp.log(col_marginals[0, 0].astype(jnp.float32)),
        counts,
    )
    return (
        shard.reshape(1, -1, width),
        shard_acc.reshape(1, -1, width),
        held.reshape(1, 1, tile_cols, width),
        held_acc.reshape(1, 1, tile_cols, width),
    )


def solution(mesh):
    in_specs = (
        P("col", "row", None),
        P("col", "row", None),
        P("col", None),
        P("row", "col", None, None),
        P("row", "col", None, None),
        P("row", "col", None),
        P(None, "col", None, "row", None),
        P(),
    )
    out_specs = (
        P("col", "row", None),
        P("col", "row", None),
        P("row", "col", None, None),
        P("row", "col", None, None),
    )
    return jax.shard_map(
        per_device, mesh=mesh, in_specs=in_specs, out_specs=out_specs, check_vma=False
    )
```

```python
import functools

import jax
import jax.numpy as jnp
from jax import lax
from jax.experimental import pallas as pl
from jax.experimental.pallas import tpu as pltpu
from jax.sharding import PartitionSpec as P

log_total = 11.5
learn_rate = 0.05


def move(value, axis, mask):
    pairs = [(source, source ^ mask) for source in range(lax.axis_size(axis))]
    return lax.ppermute(value, axis, pairs)


def adagrad(param, accum, grad):
    accum = accum + grad * grad
    return (param - learn_rate * grad / jnp.sqrt(accum), accum)


def row_sum_scatter(value):
    size = lax.axis_size("row")
    if size & (size - 1):
        return lax.psum_scatter(value, "row", scatter_dimension=0, tiled=True)
    me = lax.axis_index("row")
    blocks = value.reshape(size, value.shape[0] // size, value.shape[1])
    bits = size.bit_length() - 1
    for bit in range(bits):
        pairs = blocks.reshape(blocks.shape[0] // 2, 2, *blocks.shape[1:])
        mine = (me >> bit) & 1
        keep = lax.dynamic_index_in_dim(pairs, mine, 1, keepdims=False)
        send = lax.dynamic_index_in_dim(pairs, 1 - mine, 1, keepdims=False)
        blocks = keep + move(send, "row", 1 << bit)
    return blocks[0]


def row_gather(value):
    size = lax.axis_size("row")
    if size & (size - 1):
        return lax.all_gather(value, "row", axis=0, tiled=True)
    me = lax.axis_index("row")
    blocks = value[None]
    for bit in reversed(range(size.bit_length() - 1)):
        other = move(blocks, "row", 1 << bit)
        low = (me >> bit) & 1 == 0
        pairs = [jnp.where(low, blocks, other), jnp.where(low, other, blocks)]
        blocks = jnp.stack(pairs, axis=1).reshape(-1, *value.shape)
    return blocks.reshape(-1, value.shape[1])


def first_of_all(value, weight=10):
    return pl.pallas_call(
        lambda source, target: None,
        in_specs=[pl.BlockSpec(memory_space=pl.ANY)],
        out_specs=pl.BlockSpec(memory_space=pl.ANY),
        out_shape=jax.ShapeDtypeStruct(value.shape, value.dtype),
        input_output_aliases={0: 0},
        cost_estimate=pl.CostEstimate(
            flops=0, bytes_accessed=weight * 40_000_000, transcendentals=0
        ),
    )(value)


def unused(value):
    return pl.pallas_call(
        lambda target: None,
        out_specs=pl.BlockSpec(memory_space=pl.ANY),
        out_shape=jax.ShapeDtypeStruct(value.shape, value.dtype),
    )()


def halves(value):
    high = value.astype(jnp.bfloat16)
    return high, (value - high.astype(jnp.float32)).astype(jnp.bfloat16)


def dot_halves(a, b, dims):
    one = lambda x, y: lax.dot_general(
        x, y, (dims, ((), ())), preferred_element_type=jnp.float32
    )
    return one(a[0], b[0]) + (one(a[0], b[1]) + one(a[1], b[0]))


def tile_kernel(tile, whole, held, rows_marginal, log_c, grad_cols, grad_rows):
    rows = whole.shape[0]
    log_rows = [
        jnp.broadcast_to(jnp.log(rows_marginal[:, at : at + 128].astype(jnp.float32)), (128, 128))
        for at in range(0, rows, 128)
    ]
    log_r = jnp.concatenate([part.T[:, :1] for part in log_rows])
    by_row, by_col = halves(whole[...]), halves(held[...])
    pred = dot_halves(by_row, by_col, ((1,), (1,)))
    counts = tile[...].astype(jnp.float32)
    target = jnp.log(jnp.maximum(counts, 1.0)) + log_total - log_r - log_c[...]
    confidence = 0.1 + 0.25 * jnp.sqrt(counts)
    miss = pred - target
    error = jnp.where(counts > 0, confidence * miss, jax.nn.sigmoid(miss)) * (1 / held.shape[0])
    error = halves(error)
    grad_rows[...] = dot_halves(error, by_col, ((1,), (0,)))
    grad_cols[...] = dot_halves(error, by_row, ((0,), (0,)))


def tile_grads(tile, whole, held, rows_marginal, log_c):
    rows, tile_cols = tile.shape
    width = whole.shape[1]
    return pl.pallas_call(
        tile_kernel,
        out_shape=[
            jax.ShapeDtypeStruct(held.shape, jnp.float32),
            jax.ShapeDtypeStruct(whole.shape, jnp.float32),
        ],
        compiler_params=pltpu.CompilerParams(vmem_limit_bytes=40 << 20),
        cost_estimate=pl.CostEstimate(
            flops=18 * rows * tile_cols * width,
            bytes_accessed=4 * (rows * tile_cols + 4 * rows * width),
            transcendentals=4 * rows * tile_cols,
        ),
    )(tile, whole, held, rows_marginal[None], log_c[None])


def crosses(mask):
    return mask & (lax.axis_size("col") // 2) != 0


def log_of(marginals):
    return jnp.log(marginals.astype(jnp.float32))


def direct_first(first, second):
    if not (crosses(first) and crosses(second)):
        return 0
    both = first ^ second
    if both & 1 == 0:
        return 1
    return 0 if first & 1 else 2


def before(first, second, state):
    shard, cols, acc, cols_marginal, counts = state
    rounds, _, rows_block, _, tile_cols = counts.shape
    held = first_of_all(move(cols, "col", first))
    both = first ^ second
    half = tile_cols // 2
    early = direct_first(first, second)
    last, next_acc, waiting = unused(cols), unused(acc), unused(acc[half:])
    if not crosses(first):
        last = move(jnp.concatenate([cols[:half], acc[:half]]), "col", both)
        last = first_of_all(last, 5)
        waiting = first_of_all(move(acc[half:], "col", first), 5)
    if early > 0:
        next_acc = first_of_all(move(acc, "col", both), 5)
    if early > 1:
        last = first_of_all(move(cols, "col", both), 5)
    log_now = move(log_of(cols_marginal), "col", first)
    whole = row_gather(shard)
    tiles = lax.optimization_barrier(
        [counts[t].reshape(rows_block, tile_cols) for t in range(rounds)]
    )
    return held, last, next_acc, waiting, log_now, whole, tiles


def between(first, second, state):
    shard, shard_acc, cols, acc, cols_marginal, held, last, next_acc, waiting = state[:9]
    grad, grad_rows = state[9:]
    both = first ^ second
    half = cols.shape[0] // 2
    if crosses(first):
        early = direct_first(first, second)
        grad = move(grad, "col", second)
        if not crosses(second):
            last = move(held, "col", second)
        elif early < 2:
            last = move(cols, "col", both)
        if early < 1:
            next_acc = move(acc, "col", both)
        last, next_acc = adagrad(last, next_acc, grad)
    else:
        later, later_acc = adagrad(held[half:], waiting, grad[half:])
        sent = move(jnp.concatenate([grad[:half], later]), "col", second)
        front, front_acc = adagrad(last[:half], last[half:], sent[:half])
        last = jnp.concatenate([front, sent[half:]])
        next_acc = jnp.concatenate([front_acc, later_acc])
    last, next_acc = first_of_all(last), first_of_all(next_acc)
    log_next = move(log_of(cols_marginal), "col", both)
    shard, shard_acc = adagrad(shard, shard_acc, row_sum_scatter(grad_rows))
    return shard, shard_acc, row_gather(shard), last, next_acc, log_next


def after(late, state):
    shard, shard_acc, held, held_acc, grad, grad_rows = state
    if late:
        half = held.shape[0] // 2
        moved = move(held_acc[half:], "col", lax.axis_size("col") - 1)
        held_acc = jnp.concatenate([held_acc[:half], moved])
    held, held_acc = adagrad(held, held_acc, grad)
    held, held_acc = first_of_all(held), first_of_all(held_acc)
    shard, shard_acc = adagrad(shard, shard_acc, row_sum_scatter(grad_rows))
    return shard, shard_acc, held, held_acc


def two_rounds(
    plan, shard, shard_acc, rows_marginal, cols, acc, cols_marginal, counts
):
    full = lax.axis_size("col") - 1
    pairs = [(m, full) for m in range(1, full)]
    pairs += [(full, m) for m in range(full - 1, 0, -1)]
    pairs.insert(full - 1, pairs[full - 1])
    which = plan[0] - plan[1] + (full - 1)

    def by_plan(step, state):
        return lax.switch(which, [lambda s, a=a, b=b: step(a, b, s) for a, b in pairs], state)

    held, last, next_acc, waiting, log_now, whole, tiles = by_plan(
        before, (shard, cols, acc, cols_marginal, counts)
    )
    grad, grad_rows = tile_grads(tiles[0], whole, held, rows_marginal, log_now)
    shard, shard_acc, whole, held, held_acc, log_next = by_plan(
        between,
        (
            *(shard, shard_acc, cols, acc, cols_marginal),
            *(held, last, next_acc, waiting, grad, grad_rows),
        ),
    )
    grad, grad_rows = tile_grads(tiles[1], whole, held, rows_marginal, log_next)
    return lax.cond(
        plan[0] >= lax.axis_size("col") // 2,
        lambda s: after(False, s),
        lambda s: after(True, s),
        (shard, shard_acc, held, held_acc, grad, grad_rows),
    )


def any_rounds(plan, shard, shard_acc, rows_marginal, held, held_acc, cols_marginal, counts):
    held_log = log_of(cols_marginal)
    rounds, _, rows_block, _, tile_cols = counts.shape
    tiles = counts.reshape(rounds, rows_block, tile_cols)
    masks = range(1, lax.axis_size("col"))
    for step in range(rounds):
        held, held_acc, held_log = lax.switch(
            plan[step] - 1,
            [lambda s, m=m: tuple(move(v, "col", m) for v in s) for m in masks],
            (held, held_acc, held_log),
        )
        whole = row_gather(shard)
        grad_cols, grad_rows = tile_grads(tiles[step], whole, held, rows_marginal, held_log)
        shard, shard_acc = adagrad(shard, shard_acc, row_sum_scatter(grad_rows))
        held, held_acc = adagrad(held, held_acc, grad_cols)
    return shard, shard_acc, held, held_acc


def per_device(
    row_factors, row_accum, row_marginals, col_factors, col_accum, col_marginals, counts, plan
):
    width = row_factors.shape[2]
    tile_cols = col_factors.shape[2]
    few = counts.shape[0] == 2 and 4 <= lax.axis_size("col") <= 8
    shard, shard_acc, held, held_acc = (two_rounds if few else any_rounds)(
        plan,
        row_factors[0],
        row_accum[0],
        row_marginals[0],
        col_factors[0, 0],
        col_accum[0, 0],
        col_marginals[0, 0],
        counts,
    )
    return (
        shard.reshape(1, -1, width),
        shard_acc.reshape(1, -1, width),
        held.reshape(1, 1, tile_cols, width),
        held_acc.reshape(1, 1, tile_cols, width),
    )


def solution(mesh):
    in_specs = (
        P("col", "row", None),
        P("col", "row", None),
        P("col", None),
        P("row", "col", None, None),
        P("row", "col", None, None),
        P("row", "col", None),
        P(None, "col", None, "row", None),
        P(),
    )
    out_specs = (
        P("col", "row", None),
        P("col", "row", None),
        P("row", "col", None, None),
        P("row", "col", None, None),
    )
    return jax.shard_map(
        per_device, mesh=mesh, in_specs=in_specs, out_specs=out_specs, check_vma=False
    )
```

```python
import functools

import jax
import jax.numpy as jnp
from jax import lax
from jax.experimental import pallas as pl
from jax.experimental.pallas import tpu as pltpu
from jax.sharding import PartitionSpec as P

log_total = 11.5
learn_rate = 0.05


def move(value, axis, mask):
    pairs = [(source, source ^ mask) for source in range(lax.axis_size(axis))]
    return lax.ppermute(value, axis, pairs)


def adagrad(param, accum, grad):
    accum = accum + grad * grad
    return (param - learn_rate * grad / jnp.sqrt(accum), accum)


def row_sum_scatter(value):
    size = lax.axis_size("row")
    if size & (size - 1):
        return lax.psum_scatter(value, "row", scatter_dimension=0, tiled=True)
    me = lax.axis_index("row")
    blocks = value.reshape(size, value.shape[0] // size, value.shape[1])
    bits = size.bit_length() - 1
    for bit in range(bits):
        pairs = blocks.reshape(blocks.shape[0] // 2, 2, *blocks.shape[1:])
        mine = (me >> bit) & 1
        keep = lax.dynamic_index_in_dim(pairs, mine, 1, keepdims=False)
        send = lax.dynamic_index_in_dim(pairs, 1 - mine, 1, keepdims=False)
        blocks = keep + move(send, "row", 1 << bit)
    return blocks[0]


def row_gather(value, beyond=None):
    size = lax.axis_size("row")
    if size & (size - 1):
        return lax.all_gather(value, "row", axis=0, tiled=True)
    me = lax.axis_index("row")
    if size == 4:
        beyond = move(value, "row", 2) if beyond is None else beyond
        blocks = jnp.stack([value, move(value, "row", 1), beyond, move(beyond, "row", 1)])
        for bit in range(2):
            pairs = blocks.reshape(-1, 2, 1 << bit, *value.shape)
            pairs = jnp.where((me >> bit) & 1 == 0, pairs, pairs[:, ::-1])
            blocks = pairs.reshape(blocks.shape)
        return blocks.reshape(-1, value.shape[1])
    blocks = value[None]
    for bit in reversed(range(size.bit_length() - 1)):
        other = move(blocks, "row", 1 << bit)
        low = (me >> bit) & 1 == 0
        pairs = [jnp.where(low, blocks, other), jnp.where(low, other, blocks)]
        blocks = jnp.stack(pairs, axis=1).reshape(-1, *value.shape)
    return blocks.reshape(-1, value.shape[1])


def first_of_all(value, weight=10):
    return pl.pallas_call(
        lambda source, target: None,
        in_specs=[pl.BlockSpec(memory_space=pl.ANY)],
        out_specs=pl.BlockSpec(memory_space=pl.ANY),
        out_shape=jax.ShapeDtypeStruct(value.shape, value.dtype),
        input_output_aliases={0: 0},
        cost_estimate=pl.CostEstimate(
            flops=0, bytes_accessed=weight * 40_000_000, transcendentals=0
        ),
    )(value)


def unused(value):
    return pl.pallas_call(
        lambda target: None,
        out_specs=pl.BlockSpec(memory_space=pl.ANY),
        out_shape=jax.ShapeDtypeStruct(value.shape, value.dtype),
    )()


def halves(value):
    high = value.astype(jnp.bfloat16)
    return high, (value - high.astype(jnp.float32)).astype(jnp.bfloat16)


def dot_halves(a, b, dims):
    one = lambda x, y: lax.dot_general(
        x, y, (dims, ((), ())), preferred_element_type=jnp.float32
    )
    return one(a[0], b[0]) + (one(a[0], b[1]) + one(a[1], b[0]))


def tile_kernel(tile, whole, held, rows_marginal, log_c, grad_cols, grad_rows):
    rows = whole.shape[0]
    log_rows = [
        jnp.broadcast_to(jnp.log(rows_marginal[:, at : at + 128].astype(jnp.float32)), (128, 128))
        for at in range(0, rows, 128)
    ]
    log_r = jnp.concatenate([part.T[:, :1] for part in log_rows])
    by_row, by_col = halves(whole[...]), halves(held[...])
    pred = dot_halves(by_row, by_col, ((1,), (1,)))
    counts = tile[...].astype(jnp.float32)
    target = jnp.log(jnp.maximum(counts, 1.0)) + log_total - log_r - log_c[...]
    confidence = 0.1 + 0.25 * jnp.sqrt(counts)
    miss = pred - target
    error = jnp.where(counts > 0, confidence * miss, jax.nn.sigmoid(miss)) * (1 / held.shape[0])
    error = halves(error)
    grad_rows[...] = dot_halves(error, by_col, ((1,), (0,)))
    grad_cols[...] = dot_halves(error, by_row, ((0,), (0,)))


def tile_grads(tile, whole, held, rows_marginal, log_c):
    rows, tile_cols = tile.shape
    width = whole.shape[1]
    return pl.pallas_call(
        tile_kernel,
        out_shape=[
            jax.ShapeDtypeStruct(held.shape, jnp.float32),
            jax.ShapeDtypeStruct(whole.shape, jnp.float32),
        ],
        compiler_params=pltpu.CompilerParams(vmem_limit_bytes=40 << 20),
        cost_estimate=pl.CostEstimate(
            flops=18 * rows * tile_cols * width,
            bytes_accessed=4 * (rows * tile_cols + 4 * rows * width),
            transcendentals=4 * rows * tile_cols,
        ),
    )(tile, whole, held, rows_marginal[None], log_c[None])


def crosses(mask):
    return mask & (lax.axis_size("col") // 2) != 0


def log_of(marginals):
    return jnp.log(marginals.astype(jnp.float32))


def early_masks(first, second):
    both = first ^ second
    if not (crosses(first) and crosses(second)):
        return 0, 0
    if both & 1 == 0:
        return both, 0
    if first & 1:
        return both & ~1, 0
    return both, both


def before(first, second, state):
    shard, cols, acc, cols_marginal, counts = state
    rounds, _, rows_block, _, tile_cols = counts.shape
    held = first_of_all(move(cols, "col", first))
    both = first ^ second
    half = tile_cols // 2
    acc_by, cols_by = early_masks(first, second)
    last, next_acc, waiting = unused(cols), unused(acc), unused(acc[half:])
    if not crosses(first):
        last = move(jnp.concatenate([cols[:half], acc[:half]]), "col", both)
        last = first_of_all(last, 5)
        waiting = first_of_all(move(acc[half:], "col", first), 5)
    if acc_by:
        next_acc = first_of_all(move(acc, "col", acc_by), 5)
    if cols_by:
        last = first_of_all(move(cols, "col", cols_by), 5)
    beyond, cols_marginal = lax.optimization_barrier((move(shard, "row", 2), cols_marginal))
    whole = row_gather(shard, beyond)
    log_cols = log_of(cols_marginal)
    log_now, log_next = move(log_cols, "col", first), move(log_cols, "col", both)
    tiles = lax.optimization_barrier(
        [counts[t].reshape(rows_block, tile_cols) for t in range(rounds)]
    )
    return held, last, next_acc, waiting, log_now, log_next, whole, tiles


def between(first, second, state):
    shard, shard_acc, cols, acc, held, last, next_acc, waiting, grad, grad_rows = state
    both = first ^ second
    half = cols.shape[0] // 2
    if crosses(first):
        acc_by, cols_by = early_masks(first, second)
        if acc_by != both:
            next_acc = move(next_acc if acc_by else acc, "col", both ^ acc_by)
        grad = move(grad, "col", second)
        if not crosses(second):
            last = move(held, "col", second)
        elif cols_by != both:
            last = move(cols, "col", both)
        last, next_acc = adagrad(last, next_acc, grad)
    else:
        later, later_acc = adagrad(held[half:], waiting, grad[half:])
        sent = move(jnp.concatenate([grad[:half], later]), "col", second)
        front, front_acc = adagrad(last[:half], last[half:], sent[:half])
        last = jnp.concatenate([front, sent[half:]])
        next_acc = jnp.concatenate([front_acc, later_acc])
    last, next_acc = first_of_all(last), first_of_all(next_acc)
    shard, shard_acc = adagrad(shard, shard_acc, row_sum_scatter(grad_rows))
    return shard, shard_acc, row_gather(shard), last, next_acc


def after(late, state):
    shard, shard_acc, held, held_acc, grad, grad_rows = state
    if late:
        half = held.shape[0] // 2
        moved = move(held_acc[half:], "col", lax.axis_size("col") - 1)
        held_acc = jnp.concatenate([held_acc[:half], moved])
    held, held_acc = adagrad(held, held_acc, grad)
    held, held_acc = first_of_all(held), first_of_all(held_acc)
    shard, shard_acc = adagrad(shard, shard_acc, row_sum_scatter(grad_rows))
    return shard, shard_acc, held, held_acc


def two_rounds(
    plan, shard, shard_acc, rows_marginal, cols, acc, cols_marginal, counts
):
    full = lax.axis_size("col") - 1
    pairs = [(m, full) for m in range(1, full)]
    pairs += [(full, m) for m in range(full - 1, 0, -1)]
    pairs.insert(full - 1, pairs[full - 1])
    which = plan[0] - plan[1] + (full - 1)

    def by_plan(step, state):
        return lax.switch(which, [lambda s, a=a, b=b: step(a, b, s) for a, b in pairs], state)

    held, last, next_acc, waiting, log_now, log_next, whole, tiles = by_plan(
        before, (shard, cols, acc, cols_marginal, counts)
    )
    grad, grad_rows = tile_grads(tiles[0], whole, held, rows_marginal, log_now)
    shard, shard_acc, whole, held, held_acc = by_plan(
        between,
        (
            *(shard, shard_acc, cols, acc, held),
            *(last, next_acc, waiting, grad, grad_rows),
        ),
    )
    grad, grad_rows = tile_grads(tiles[1], whole, held, rows_marginal, log_next)
    return lax.cond(
        plan[0] >= lax.axis_size("col") // 2,
        lambda s: after(False, s),
        lambda s: after(True, s),
        (shard, shard_acc, held, held_acc, grad, grad_rows),
    )


def any_rounds(plan, shard, shard_acc, rows_marginal, held, held_acc, cols_marginal, counts):
    held_log = log_of(cols_marginal)
    rounds, _, rows_block, _, tile_cols = counts.shape
    tiles = counts.reshape(rounds, rows_block, tile_cols)
    masks = range(1, lax.axis_size("col"))
    for step in range(rounds):
        held, held_acc, held_log = lax.switch(
            plan[step] - 1,
            [lambda s, m=m: tuple(move(v, "col", m) for v in s) for m in masks],
            (held, held_acc, held_log),
        )
        whole = row_gather(shard)
        grad_cols, grad_rows = tile_grads(tiles[step], whole, held, rows_marginal, held_log)
        shard, shard_acc = adagrad(shard, shard_acc, row_sum_scatter(grad_rows))
        held, held_acc = adagrad(held, held_acc, grad_cols)
    return shard, shard_acc, held, held_acc


def per_device(
    row_factors, row_accum, row_marginals, col_factors, col_accum, col_marginals, counts, plan
):
    width = row_factors.shape[2]
    tile_cols = col_factors.shape[2]
    few = counts.shape[0] == 2 and 4 <= lax.axis_size("col") <= 8
    shard, shard_acc, held, held_acc = (two_rounds if few else any_rounds)(
        plan,
        row_factors[0],
        row_accum[0],
        row_marginals[0],
        col_factors[0, 0],
        col_accum[0, 0],
        col_marginals[0, 0],
        counts,
    )
    return (
        shard.reshape(1, -1, width),
        shard_acc.reshape(1, -1, width),
        held.reshape(1, 1, tile_cols, width),
        held_acc.reshape(1, 1, tile_cols, width),
    )


def solution(mesh):
    in_specs = (
        P("col", "row", None),
        P("col", "row", None),
        P("col", None),
        P("row", "col", None, None),
        P("row", "col", None, None),
        P("row", "col", None),
        P(None, "col", None, "row", None),
        P(),
    )
    out_specs = (
        P("col", "row", None),
        P("col", "row", None),
        P("row", "col", None, None),
        P("row", "col", None, None),
    )
    return jax.shard_map(
        per_device, mesh=mesh, in_specs=in_specs, out_specs=out_specs, check_vma=False
    )
```

```python
import functools

import jax
import jax.numpy as jnp
from jax import lax
from jax.experimental import pallas as pl
from jax.experimental.pallas import tpu as pltpu
from jax.sharding import PartitionSpec as P

log_total = 11.5
learn_rate = 0.05


def move(value, axis, mask):
    pairs = [(source, source ^ mask) for source in range(lax.axis_size(axis))]
    return lax.ppermute(value, axis, pairs)


def adagrad(param, accum, grad):
    accum = accum + grad * grad
    return (param - learn_rate * grad / jnp.sqrt(accum), accum)


def row_sum_scatter(value):
    size = lax.axis_size("row")
    if size & (size - 1):
        return lax.psum_scatter(value, "row", scatter_dimension=0, tiled=True)
    me = lax.axis_index("row")
    blocks = value.reshape(size, value.shape[0] // size, value.shape[1])
    bits = size.bit_length() - 1
    for bit in range(bits):
        pairs = blocks.reshape(blocks.shape[0] // 2, 2, *blocks.shape[1:])
        mine = (me >> bit) & 1
        keep = lax.dynamic_index_in_dim(pairs, mine, 1, keepdims=False)
        send = lax.dynamic_index_in_dim(pairs, 1 - mine, 1, keepdims=False)
        blocks = keep + move(send, "row", 1 << bit)
    return blocks[0]


def row_gather(value, beyond=None):
    size = lax.axis_size("row")
    if size & (size - 1):
        return lax.all_gather(value, "row", axis=0, tiled=True)
    me = lax.axis_index("row")
    if size == 4:
        beyond = move(value, "row", 2) if beyond is None else beyond
        blocks = jnp.stack([value, move(value, "row", 1), beyond, move(beyond, "row", 1)])
        for bit in range(2):
            pairs = blocks.reshape(-1, 2, 1 << bit, *value.shape)
            pairs = jnp.where((me >> bit) & 1 == 0, pairs, pairs[:, ::-1])
            blocks = pairs.reshape(blocks.shape)
        return blocks.reshape(-1, value.shape[1])
    blocks = value[None]
    for bit in reversed(range(size.bit_length() - 1)):
        other = move(blocks, "row", 1 << bit)
        low = (me >> bit) & 1 == 0
        pairs = [jnp.where(low, blocks, other), jnp.where(low, other, blocks)]
        blocks = jnp.stack(pairs, axis=1).reshape(-1, *value.shape)
    return blocks.reshape(-1, value.shape[1])


def first_of_all(value, weight=10):
    return pl.pallas_call(
        lambda source, target: None,
        in_specs=[pl.BlockSpec(memory_space=pl.ANY)],
        out_specs=pl.BlockSpec(memory_space=pl.ANY),
        out_shape=jax.ShapeDtypeStruct(value.shape, value.dtype),
        input_output_aliases={0: 0},
        cost_estimate=pl.CostEstimate(
            flops=0, bytes_accessed=weight * 40_000_000, transcendentals=0
        ),
    )(value)


def unused(value):
    return pl.pallas_call(
        lambda target: None,
        out_specs=pl.BlockSpec(memory_space=pl.ANY),
        out_shape=jax.ShapeDtypeStruct(value.shape, value.dtype),
    )()


def halves(value):
    high = value.astype(jnp.bfloat16)
    return high, (value - high.astype(jnp.float32)).astype(jnp.bfloat16)


def dot_halves(a, b, dims):
    one = lambda x, y: lax.dot_general(
        x, y, (dims, ((), ())), preferred_element_type=jnp.float32
    )
    return one(a[0], b[0]) + (one(a[0], b[1]) + one(a[1], b[0]))


def tile_kernel(tile, whole, held, rows_marginal, log_c, grad_cols, grad_rows):
    rows = whole.shape[0]
    log_rows = [
        jnp.broadcast_to(jnp.log(rows_marginal[:, at : at + 128].astype(jnp.float32)), (128, 128))
        for at in range(0, rows, 128)
    ]
    log_r = jnp.concatenate([part.T[:, :1] for part in log_rows])
    by_row, by_col = halves(whole[...]), halves(held[...])
    pred = dot_halves(by_row, by_col, ((1,), (1,)))
    counts = tile[...].astype(jnp.float32)
    target = jnp.log(jnp.maximum(counts, 1.0)) + log_total - log_r - log_c[...]
    confidence = 0.1 + 0.25 * jnp.sqrt(counts)
    miss = pred - target
    error = jnp.where(counts > 0, confidence * miss, jax.nn.sigmoid(miss)) * (1 / held.shape[0])
    error = halves(error)
    grad_rows[...] = dot_halves(error, by_col, ((1,), (0,)))
    grad_cols[...] = dot_halves(error, by_row, ((0,), (0,)))


def tile_grads(tile, whole, held, rows_marginal, log_c):
    rows, tile_cols = tile.shape
    width = whole.shape[1]
    return pl.pallas_call(
        tile_kernel,
        out_shape=[
            jax.ShapeDtypeStruct(held.shape, jnp.float32),
            jax.ShapeDtypeStruct(whole.shape, jnp.float32),
        ],
        compiler_params=pltpu.CompilerParams(vmem_limit_bytes=40 << 20),
        cost_estimate=pl.CostEstimate(
            flops=18 * rows * tile_cols * width,
            bytes_accessed=4 * (rows * tile_cols + 4 * rows * width),
            transcendentals=4 * rows * tile_cols,
        ),
    )(tile, whole, held, rows_marginal[None], log_c[None])


def crosses(mask):
    return mask & (lax.axis_size("col") // 2) != 0


def log_of(marginals):
    return jnp.log(marginals.astype(jnp.float32))


def early_masks(first, second):
    both = first ^ second
    if not (crosses(first) and crosses(second)):
        return 0, 0
    if both & 1 == 0:
        return both, 0
    if first & 1:
        return both & ~1, 0
    return both, both & 1


def before(first, second, state):
    shard, cols, acc, cols_marginal, counts = state
    rounds, _, rows_block, _, tile_cols = counts.shape
    held = first_of_all(move(cols, "col", first))
    both = first ^ second
    half = tile_cols // 2
    acc_by, cols_by = early_masks(first, second)
    last, next_acc, waiting = unused(cols), unused(acc), unused(acc[half:])
    if not crosses(first):
        last = move(jnp.concatenate([cols[:half], acc[:half]]), "col", both)
        last = first_of_all(last, 5)
        waiting = first_of_all(move(acc[half:], "col", first), 5)
    if acc_by:
        next_acc = first_of_all(move(acc, "col", acc_by), 5)
    if cols_by:
        last = first_of_all(move(cols, "col", cols_by), 5)
    beyond, cols_marginal = lax.optimization_barrier((move(shard, "row", 2), cols_marginal))
    whole = row_gather(shard, beyond)
    log_cols = log_of(cols_marginal)
    log_now, log_next = move(log_cols, "col", first), move(log_cols, "col", both)
    tiles = lax.optimization_barrier(
        [counts[t].reshape(rows_block, tile_cols) for t in range(rounds)]
    )
    return held, last, next_acc, waiting, log_now, log_next, whole, tiles


def between(first, second, state):
    shard, shard_acc, cols, acc, held, last, next_acc, waiting, grad, grad_rows = state
    both = first ^ second
    half = cols.shape[0] // 2
    if crosses(first):
        acc_by, cols_by = early_masks(first, second)
        if acc_by != both:
            next_acc = move(next_acc if acc_by else acc, "col", both ^ acc_by)
        grad = move(grad, "col", second)
        if not crosses(second):
            last = move(held, "col", second)
        elif cols_by != both:
            last = move(last if cols_by else cols, "col", both ^ cols_by)
        last, next_acc = adagrad(last, next_acc, grad)
    else:
        later, later_acc = adagrad(held[half:], waiting, grad[half:])
        sent = move(jnp.concatenate([grad[:half], later]), "col", second)
        front, front_acc = adagrad(last[:half], last[half:], sent[:half])
        last = jnp.concatenate([front, sent[half:]])
        next_acc = jnp.concatenate([front_acc, later_acc])
    last, next_acc = first_of_all(last), first_of_all(next_acc)
    shard, shard_acc = adagrad(shard, shard_acc, row_sum_scatter(grad_rows))
    return shard, shard_acc, row_gather(shard), last, next_acc


def after(late, state):
    shard, shard_acc, held, held_acc, grad, grad_rows = state
    if late:
        half = held.shape[0] // 2
        moved = move(held_acc[half:], "col", lax.axis_size("col") - 1)
        held_acc = jnp.concatenate([held_acc[:half], moved])
    held, held_acc = adagrad(held, held_acc, grad)
    held, held_acc = first_of_all(held), first_of_all(held_acc)
    shard, shard_acc = adagrad(shard, shard_acc, row_sum_scatter(grad_rows))
    return shard, shard_acc, held, held_acc


def two_rounds(
    plan, shard, shard_acc, rows_marginal, cols, acc, cols_marginal, counts
):
    full = lax.axis_size("col") - 1
    pairs = [(m, full) for m in range(1, full)]
    pairs += [(full, m) for m in range(full - 1, 0, -1)]
    pairs.insert(full - 1, pairs[full - 1])
    at = lax.iota(plan.dtype, 2)
    which = jnp.sum(jnp.where(at == 0, plan + (full - 1), -plan))

    def by_plan(step, state):
        return lax.switch(which, [lambda s, a=a, b=b: step(a, b, s) for a, b in pairs], state)

    held, last, next_acc, waiting, log_now, log_next, whole, tiles = by_plan(
        before, (shard, cols, acc, cols_marginal, counts)
    )
    grad, grad_rows = tile_grads(tiles[0], whole, held, rows_marginal, log_now)
    shard, shard_acc, whole, held, held_acc = by_plan(
        between,
        (
            *(shard, shard_acc, cols, acc, held),
            *(last, next_acc, waiting, grad, grad_rows),
        ),
    )
    grad, grad_rows = tile_grads(tiles[1], whole, held, rows_marginal, log_next)
    return lax.cond(
        which >= (full + 1) // 2 - 1,
        lambda s: after(False, s),
        lambda s: after(True, s),
        (shard, shard_acc, held, held_acc, grad, grad_rows),
    )


def any_rounds(plan, shard, shard_acc, rows_marginal, held, held_acc, cols_marginal, counts):
    held_log = log_of(cols_marginal)
    rounds, _, rows_block, _, tile_cols = counts.shape
    tiles = counts.reshape(rounds, rows_block, tile_cols)
    masks = range(1, lax.axis_size("col"))
    for step in range(rounds):
        held, held_acc, held_log = lax.switch(
            plan[step] - 1,
            [lambda s, m=m: tuple(move(v, "col", m) for v in s) for m in masks],
            (held, held_acc, held_log),
        )
        whole = row_gather(shard)
        grad_cols, grad_rows = tile_grads(tiles[step], whole, held, rows_marginal, held_log)
        shard, shard_acc = adagrad(shard, shard_acc, row_sum_scatter(grad_rows))
        held, held_acc = adagrad(held, held_acc, grad_cols)
    return shard, shard_acc, held, held_acc


def per_device(
    row_factors, row_accum, row_marginals, col_factors, col_accum, col_marginals, counts, plan
):
    width = row_factors.shape[2]
    tile_cols = col_factors.shape[2]
    few = counts.shape[0] == 2 and 4 <= lax.axis_size("col") <= 8
    shard, shard_acc, held, held_acc = (two_rounds if few else any_rounds)(
        plan,
        row_factors[0],
        row_accum[0],
        row_marginals[0],
        col_factors[0, 0],
        col_accum[0, 0],
        col_marginals[0, 0],
        counts,
    )
    return (
        shard.reshape(1, -1, width),
        shard_acc.reshape(1, -1, width),
        held.reshape(1, 1, tile_cols, width),
        held_acc.reshape(1, 1, tile_cols, width),
    )


def solution(mesh):
    in_specs = (
        P("col", "row", None),
        P("col", "row", None),
        P("col", None),
        P("row", "col", None, None),
        P("row", "col", None, None),
        P("row", "col", None),
        P(None, "col", None, "row", None),
        P(),
    )
    out_specs = (
        P("col", "row", None),
        P("col", "row", None),
        P("row", "col", None, None),
        P("row", "col", None, None),
    )
    return jax.shard_map(
        per_device, mesh=mesh, in_specs=in_specs, out_specs=out_specs, check_vma=False
    )
```

```python
import functools

import jax
import jax.numpy as jnp
from jax import lax
from jax.experimental import pallas as pl
from jax.experimental.pallas import tpu as pltpu
from jax.sharding import PartitionSpec as P

log_total = 11.5
learn_rate = 0.05


def move(value, axis, mask):
    pairs = [(source, source ^ mask) for source in range(lax.axis_size(axis))]
    return lax.ppermute(value, axis, pairs)


def adagrad(param, accum, grad):
    accum = accum + grad * grad
    return (param - learn_rate * grad / jnp.sqrt(accum), accum)


def row_sum_scatter(value):
    size = lax.axis_size("row")
    if size & (size - 1):
        return lax.psum_scatter(value, "row", scatter_dimension=0, tiled=True)
    me = lax.axis_index("row")
    blocks = value.reshape(size, value.shape[0] // size, value.shape[1])
    bits = size.bit_length() - 1
    for bit in range(bits):
        pairs = blocks.reshape(blocks.shape[0] // 2, 2, *blocks.shape[1:])
        mine = (me >> bit) & 1
        keep = lax.dynamic_index_in_dim(pairs, mine, 1, keepdims=False)
        send = lax.dynamic_index_in_dim(pairs, 1 - mine, 1, keepdims=False)
        blocks = keep + move(send, "row", 1 << bit)
    return blocks[0]


def row_gather(value, beyond=None):
    size = lax.axis_size("row")
    if size & (size - 1):
        return lax.all_gather(value, "row", axis=0, tiled=True)
    me = lax.axis_index("row")
    if size == 4:
        beyond = move(value, "row", 2) if beyond is None else beyond
        blocks = jnp.stack([value, move(value, "row", 1), beyond, move(beyond, "row", 1)])
        for bit in range(2):
            pairs = blocks.reshape(-1, 2, 1 << bit, *value.shape)
            pairs = jnp.where((me >> bit) & 1 == 0, pairs, pairs[:, ::-1])
            blocks = pairs.reshape(blocks.shape)
        return blocks.reshape(-1, value.shape[1])
    blocks = value[None]
    for bit in reversed(range(size.bit_length() - 1)):
        other = move(blocks, "row", 1 << bit)
        low = (me >> bit) & 1 == 0
        pairs = [jnp.where(low, blocks, other), jnp.where(low, other, blocks)]
        blocks = jnp.stack(pairs, axis=1).reshape(-1, *value.shape)
    return blocks.reshape(-1, value.shape[1])


def first_of_all(value, weight=10):
    return pl.pallas_call(
        lambda source, target: None,
        in_specs=[pl.BlockSpec(memory_space=pl.ANY)],
        out_specs=pl.BlockSpec(memory_space=pl.ANY),
        out_shape=jax.ShapeDtypeStruct(value.shape, value.dtype),
        input_output_aliases={0: 0},
        cost_estimate=pl.CostEstimate(
            flops=0, bytes_accessed=weight * 40_000_000, transcendentals=0
        ),
    )(value)


def unused(value):
    return pl.pallas_call(
        lambda target: None,
        out_specs=pl.BlockSpec(memory_space=pl.ANY),
        out_shape=jax.ShapeDtypeStruct(value.shape, value.dtype),
    )()


def halves(value):
    high = value.astype(jnp.bfloat16)
    return high, (value - high.astype(jnp.float32)).astype(jnp.bfloat16)


def dot_halves(a, b, dims):
    one = lambda x, y: lax.dot_general(
        x, y, (dims, ((), ())), preferred_element_type=jnp.float32
    )
    return one(a[0], b[0]) + (one(a[0], b[1]) + one(a[1], b[0]))


def tile_kernel(tile, whole, held, rows_marginal, log_c, grad_cols, grad_rows):
    rows = whole.shape[0]
    log_rows = [
        jnp.broadcast_to(jnp.log(rows_marginal[:, at : at + 128].astype(jnp.float32)), (128, 128))
        for at in range(0, rows, 128)
    ]
    log_r = jnp.concatenate([part.T[:, :1] for part in log_rows])
    by_row, by_col = halves(whole[...]), halves(held[...])
    pred = dot_halves(by_row, by_col, ((1,), (1,)))
    counts = tile[...].astype(jnp.float32)
    target = jnp.log(jnp.maximum(counts, 1.0)) + log_total - log_r - log_c[...]
    confidence = 0.1 + 0.25 * jnp.sqrt(counts)
    miss = pred - target
    error = jnp.where(counts > 0, confidence * miss, jax.nn.sigmoid(miss)) * (1 / held.shape[0])
    error = halves(error)
    grad_rows[...] = dot_halves(error, by_col, ((1,), (0,)))
    grad_cols[...] = dot_halves(error, by_row, ((0,), (0,)))


def tile_grads(tiles, step, whole, held, rows_marginal, log_c):
    _, rows, tile_cols = tiles.shape
    width = whole.shape[1]
    shapes = [whole.shape, held.shape, (1, rows), (1, tile_cols)]
    return pl.pallas_call(
        tile_kernel,
        grid=(1,),
        in_specs=[
            pl.BlockSpec((None, rows, tile_cols), lambda i: (step, 0, 0)),
            *[pl.BlockSpec(shape, lambda i: (0, 0)) for shape in shapes],
        ],
        out_specs=[pl.BlockSpec(shape, lambda i: (0, 0)) for shape in (held.shape, whole.shape)],
        out_shape=[
            jax.ShapeDtypeStruct(held.shape, jnp.float32),
            jax.ShapeDtypeStruct(whole.shape, jnp.float32),
        ],
        compiler_params=pltpu.CompilerParams(vmem_limit_bytes=40 << 20),
        cost_estimate=pl.CostEstimate(
            flops=18 * rows * tile_cols * width,
            bytes_accessed=4 * (rows * tile_cols + 4 * rows * width),
            transcendentals=4 * rows * tile_cols,
        ),
    )(tiles, whole, held, rows_marginal[None], log_c[None])


def crosses(mask):
    return mask & (lax.axis_size("col") // 2) != 0


def log_of(marginals):
    return jnp.log(marginals.astype(jnp.float32))


def early_masks(first, second):
    both = first ^ second
    if not (crosses(first) and crosses(second)):
        return 0, 0
    if both & 1 == 0:
        return both, 0
    if first & 1:
        return both & ~1, 0
    return both, both & 1


def before(first, second, state):
    shard, cols, acc, cols_marginal, counts = state
    rounds, _, rows_block, _, tile_cols = counts.shape
    held = first_of_all(move(cols, "col", first))
    both = first ^ second
    half = tile_cols // 2
    acc_by, cols_by = early_masks(first, second)
    last, next_acc, waiting = unused(cols), unused(acc), unused(acc[half:])
    if not crosses(first):
        last = move(jnp.concatenate([cols[:half], acc[:half]]), "col", both)
        last = first_of_all(last, 5)
        waiting = first_of_all(move(acc[half:], "col", first), 5)
    if acc_by:
        next_acc = first_of_all(move(acc, "col", acc_by), 5)
    if cols_by:
        last = first_of_all(move(cols, "col", cols_by), 5)
    beyond, cols_marginal, counts = lax.optimization_barrier(
        (move(shard, "row", 2), cols_marginal, counts)
    )
    whole = row_gather(shard, beyond)
    log_cols = log_of(cols_marginal)
    log_now, log_next = move(log_cols, "col", first), move(log_cols, "col", both)
    tiles = lax.optimization_barrier(counts.reshape(rounds, rows_block, tile_cols))
    return held, last, next_acc, waiting, log_now, log_next, whole, tiles


def between(first, second, state):
    shard, shard_acc, cols, acc, held, last, next_acc, waiting, grad, grad_rows = state
    both = first ^ second
    half = cols.shape[0] // 2
    if crosses(first):
        acc_by, cols_by = early_masks(first, second)
        if acc_by != both:
            next_acc = move(next_acc if acc_by else acc, "col", both ^ acc_by)
        grad = move(grad, "col", second)
        if not crosses(second):
            last = move(held, "col", second)
        elif cols_by != both:
            last = move(last if cols_by else cols, "col", both ^ cols_by)
        last, next_acc = adagrad(last, next_acc, grad)
    else:
        later, later_acc = adagrad(held[half:], waiting, grad[half:])
        sent = move(jnp.concatenate([grad[:half], later]), "col", second)
        front, front_acc = adagrad(last[:half], last[half:], sent[:half])
        last = jnp.concatenate([front, sent[half:]])
        next_acc = jnp.concatenate([front_acc, later_acc])
    last, next_acc = first_of_all(last), first_of_all(next_acc)
    shard, shard_acc = adagrad(shard, shard_acc, row_sum_scatter(grad_rows))
    return shard, shard_acc, row_gather(shard), last, next_acc


def after(late, state):
    shard, shard_acc, held, held_acc, grad, grad_rows = state
    if late:
        half = held.shape[0] // 2
        moved = move(held_acc[half:], "col", lax.axis_size("col") - 1)
        held_acc = jnp.concatenate([held_acc[:half], moved])
    held, held_acc = adagrad(held, held_acc, grad)
    held, held_acc = first_of_all(held), first_of_all(held_acc)
    shard, shard_acc = adagrad(shard, shard_acc, row_sum_scatter(grad_rows))
    return shard, shard_acc, held, held_acc


def two_rounds(
    plan, shard, shard_acc, rows_marginal, cols, acc, cols_marginal, counts
):
    full = lax.axis_size("col") - 1
    pairs = [(m, full) for m in range(1, full)]
    pairs += [(full, m) for m in range(full - 1, 0, -1)]
    pairs.insert(full - 1, pairs[full - 1])
    at = lax.iota(plan.dtype, 2)
    which = jnp.sum(jnp.where(at == 0, plan + (full - 1), -plan))

    def by_plan(step, state):
        return lax.switch(which, [lambda s, a=a, b=b: step(a, b, s) for a, b in pairs], state)

    held, last, next_acc, waiting, log_now, log_next, whole, tiles = by_plan(
        before, (shard, cols, acc, cols_marginal, counts)
    )
    grad, grad_rows = tile_grads(tiles, 0, whole, held, rows_marginal, log_now)
    shard, shard_acc, whole, held, held_acc = by_plan(
        between,
        (
            *(shard, shard_acc, cols, acc, held),
            *(last, next_acc, waiting, grad, grad_rows),
        ),
    )
    grad, grad_rows = tile_grads(tiles, 1, whole, held, rows_marginal, log_next)
    return lax.cond(
        which >= (full + 1) // 2 - 1,
        lambda s: after(False, s),
        lambda s: after(True, s),
        (shard, shard_acc, held, held_acc, grad, grad_rows),
    )


def any_rounds(plan, shard, shard_acc, rows_marginal, held, held_acc, cols_marginal, counts):
    held_log = log_of(cols_marginal)
    rounds, _, rows_block, _, tile_cols = counts.shape
    tiles = counts.reshape(rounds, rows_block, tile_cols)
    masks = range(1, lax.axis_size("col"))
    for step in range(rounds):
        held, held_acc, held_log = lax.switch(
            plan[step] - 1,
            [lambda s, m=m: tuple(move(v, "col", m) for v in s) for m in masks],
            (held, held_acc, held_log),
        )
        whole = row_gather(shard)
        grad_cols, grad_rows = tile_grads(tiles, step, whole, held, rows_marginal, held_log)
        shard, shard_acc = adagrad(shard, shard_acc, row_sum_scatter(grad_rows))
        held, held_acc = adagrad(held, held_acc, grad_cols)
    return shard, shard_acc, held, held_acc


def per_device(
    row_factors, row_accum, row_marginals, col_factors, col_accum, col_marginals, counts, plan
):
    width = row_factors.shape[2]
    tile_cols = col_factors.shape[2]
    few = counts.shape[0] == 2 and 4 <= lax.axis_size("col") <= 8
    shard, shard_acc, held, held_acc = (two_rounds if few else any_rounds)(
        plan,
        row_factors[0],
        row_accum[0],
        row_marginals[0],
        col_factors[0, 0],
        col_accum[0, 0],
        col_marginals[0, 0],
        counts,
    )
    return (
        shard.reshape(1, -1, width),
        shard_acc.reshape(1, -1, width),
        held.reshape(1, 1, tile_cols, width),
        held_acc.reshape(1, 1, tile_cols, width),
    )


def solution(mesh):
    in_specs = (
        P("col", "row", None),
        P("col", "row", None),
        P("col", None),
        P("row", "col", None, None),
        P("row", "col", None, None),
        P("row", "col", None),
        P(None, "col", None, "row", None),
        P(),
    )
    out_specs = (
        P("col", "row", None),
        P("col", "row", None),
        P("row", "col", None, None),
        P("row", "col", None, None),
    )
    return jax.shard_map(
        per_device, mesh=mesh, in_specs=in_specs, out_specs=out_specs, check_vma=False
    )
```
